256 devices in a mesh: fsdp: 8 (over z), expert: 32 (over y, x, core).
Axes of the slice: x: 4, y: 4, z: 8, core: 2. Of those that a mesh axis runs over, the one named last changes fastest.
Arguments:
- tokens: bfloat16 [12288, 4096], P(('fsdp', 'expert')), may hold values from -6 to 6
- expert_ids: int32 [12288, 8], P(('fsdp', 'expert')), may hold values from 0 to 31, all different within a row; in each aligned block of 48 rows (0 to 47, 48 to 95, ...) at most 18 rows name the same one
- gate_scale: float32 [12288, 8], P(('fsdp', 'expert')), may hold values from 0.05 to 0.5
- gate_up: bfloat16 [32, 4096, 1536], P('expert', 'fsdp'), may hold values from -0.09375 to 0.09375
- down: bfloat16 [32, 768, 4096], P('expert', 'fsdp'), may hold values from -0.21875 to 0.21875
Outputs:
- combined: bfloat16 [12288, 4096], P(('fsdp', 'expert'))
The draws below stay inside these ranges and needn't reach their ends.
Inputs may be any that keep to these rules, and one draw needn't show every extreme that they name: `expert_ids`: each row names 8 different experts. Within each aligned block of 48 tokens (the rows of one device) no expert is named by more than 18 rows, and in every draw some expert is named by exactly 18 rows of some block.
All inputs are finite; a program needn't handle non-finite values.
Results may differ from the reference program's by a relative error of at most 0.0057.
Values may be sent and summed in bfloat16 or wider, within the bound.
No kernel may reach another device: no remote copies, remote signals or barrier semaphores. Data moves between devices by JAX's collectives and lax.ppermute only.
A program may use at most 128 MiB of HBM per device.

```python
import math
import jax
import jax.numpy as jnp
import numpy as np
from jax import lax

D = 4096
FF = 768
EXPERTS = 32
TOP = 8
TOK_DEV = 48
CAP = 18
TOKENS = 12288


def shard_levels(rng, dims, cuts, smallest, top_value):
    gain, own = 1.0, jax.random.fold_in(rng, 6)
    for dim, shards_of in cuts:
        draws = jnp.exp(jax.random.uniform(jax.random.fold_in(own, dim), (shards_of,), jnp.float32, smallest / len(cuts), top_value / len(cuts)))
        gain = gain * jnp.repeat(draws, dims[dim] // shards_of).reshape([-1 if axis == dim else 1 for axis in range(len(dims))])
    return gain


def deal_out(own_key, own, number, rows, count, top, reach, lean):
    sequence = jax.random.permutation(own_key, count)
    crowded, common = load_shares(count, rows * top, reach, lean, True), load_shares(count, rows * top, reach, lean, False)
    places = jnp.arange(count)

    def named(lengths, rotation):
        used = int((lengths > 0).sum())
        fixed = max(1, used // 4)
        shifted = fixed + (places - fixed + rotation * (used - fixed)) % max(1, count - fixed)
        return jnp.zeros((count,), jnp.int32).at[sequence[jnp.where(places < fixed, places, shifted)]].set(jnp.asarray(lengths, jnp.int32))

    lengths = jnp.where(number % 4 == 0, named(crowded, number // 4), named(common, number - number // 4 - 1))
    mixed = jax.random.permutation(jax.random.fold_in(own, 3), count)
    donor, taker = mixed[0:count // 2 * 2:2], mixed[1:count // 2 * 2:2]
    margin = jnp.minimum(lengths[donor] - 1, reach - lengths[taker]) // 2
    margin = jnp.where((donor == sequence[0]) | (taker == sequence[0]) | (lengths[taker] == 0), 0, jnp.maximum(margin, 0))
    shifted = jax.random.randint(jax.random.fold_in(own, 4), (count // 2,), 0, 1 << 20) % (margin + 1)
    lengths = lengths.at[donor].add(-shifted).at[taker].add(shifted)
    members = jnp.searchsorted(jnp.cumsum(lengths), jnp.arange(rows * top), side="right").astype(jnp.int32)
    table = members.reshape(top, rows).T
    table = table[jax.random.permutation(jax.random.fold_in(own, 1), rows)]
    rotation = jax.random.randint(jax.random.fold_in(own, 2), (rows, 1), 0, top)
    return jnp.take_along_axis(table, (jnp.arange(top)[None, :] + rotation) % top, axis=1)


def load_shares(amount, total, bound, slope, full):
    portions = [(1 << 20) // math.isqrt(grade ** slope) + 1 for grade in range(1, amount + 1)]
    largest = bound if full else min(bound, max(-(-total // amount), total * portions[0] // sum(portions)))
    least = 1 if total - largest >= amount - 1 else 0
    holding, surplus = [largest] + [least] * (amount - 1), total - largest - least * (amount - 1)
    while surplus > 0:
        candidates = [i for i in range(1, amount) if holding[i] < largest] or [i for i in range(1, amount) if holding[i] < bound]
        mass, left = sum([portions[i] for i in candidates]), surplus
        for i in candidates:
            extra = min(bound - holding[i], max(1, left * portions[i] // mass), surplus)
            holding[i] = holding[i] + extra
            surplus = surplus - extra
    return np.array(holding)


def centred(key, dims, deviation, most, shards=(), held_as=jnp.bfloat16):
    values = deviation * jax.random.normal(key, dims, jnp.float32)
    if shards:
        values = values * shard_levels(key, dims, shards, -0.22, 0.18)
    return jnp.clip(values, -most, most).astype(held_as)


def setup_inputs(seed: int = 0) -> dict:
    splits = jax.random.split(jax.random.key(seed), 6)
    tokens = centred(splits[0], (TOKENS, D), 1.0, 6.0, ((0, 256),))
    expert_ids_keys = jax.random.split(jax.random.fold_in(splits[1], 1), TOKENS // TOK_DEV)
    expert_ids_turns = jax.random.permutation(jax.random.fold_in(splits[1], 3), TOKENS // TOK_DEV)
    expert_ids = jax.vmap(lambda own, number: deal_out(jax.random.fold_in(splits[1], 2), own, number, TOK_DEV, EXPERTS, TOP, CAP, 2))(expert_ids_keys, expert_ids_turns).reshape((TOKENS, TOP))
    gate_scale = jnp.clip(jnp.exp(math.log(0.5) - 2.3025851 * jax.random.uniform(splits[2], (TOKENS, TOP), jnp.float32) ** shard_levels(splits[2], (TOKENS, TOP), ((0, 256),), -0.2, 0.2)), 0.05, 0.5)
    gate_up = centred(splits[3], (EXPERTS, D, 2 * FF), D ** -0.5, 0.09375, ((0, 32), (1, 8)))
    down = centred(splits[4], (EXPERTS, FF, D), FF ** -0.5, 0.21875, ((0, 32), (1, 8)))
    return {"tokens": tokens, "expert_ids": expert_ids, "gate_scale": gate_scale, "gate_up": gate_up, "down": down}


def reference(tokens, expert_ids, gate_scale, gate_up, down):
    blocks = TOKENS // TOK_DEV
    grouped = expert_ids.reshape(blocks, TOK_DEV * TOP)
    onehot = (grouped[:, :, None] == jnp.arange(EXPERTS, dtype=jnp.int32)[None, None, :]).astype(jnp.int32)
    before = jnp.cumsum(onehot, axis=1) - onehot
    slot_index = jnp.sum(before * onehot, axis=2).astype(jnp.int32)
    block_index = jnp.arange(blocks, dtype=jnp.int32)[:, None]
    flat_place = (grouped * (blocks * CAP) + block_index * CAP + slot_index).reshape(-1)
    token_of = (block_index * TOK_DEV + jnp.arange(TOK_DEV * TOP, dtype=jnp.int32)[None, :] // TOP).reshape(-1)
    token_index = jnp.full((EXPERTS * blocks * CAP,), TOKENS, jnp.int32).at[flat_place].set(token_of)
    token_index = token_index.reshape(EXPERTS, blocks * CAP)
    weight_table = jnp.zeros((EXPERTS * blocks * CAP,), jnp.float32).at[flat_place].set(gate_scale.reshape(-1))
    weight_table = weight_table.reshape(EXPERTS, blocks * CAP)
    padded = jnp.concatenate([tokens, jnp.zeros((1, D), tokens.dtype)], axis=0)

    def one_expert(total, inputs):
        weights_in, weights_out, rows_index, row_scale = inputs
        rows = padded[rows_index]
        both = jnp.dot(rows, weights_in, preferred_element_type=jnp.float32)
        hidden = (jax.nn.silu(both[:, :FF]) * both[:, FF:]).astype(jnp.bfloat16)
        result = jnp.dot(hidden, weights_out, preferred_element_type=jnp.float32).astype(jnp.bfloat16)
        total = total.at[rows_index].add(row_scale[:, None] * result.astype(jnp.float32))
        return total, None

    total = jnp.zeros((TOKENS + 1, D), jnp.float32)
    total, _ = lax.scan(one_expert, total, (gate_up, down, token_index, weight_table))
    return total[:TOKENS].astype(jnp.bfloat16)
```

```python
import functools

import jax
import jax.numpy as jnp
from jax import lax
from jax.experimental import pallas as pl
from jax.experimental.pallas import tpu as pltpu
from jax.sharding import PartitionSpec as P

FF = 768
EXPERTS = 32
CAP = 18
MAIN = 16
SPILL = CAP - MAIN
LANES = 128
MIB = 1024 * 1024


def iota(shape, axis):
    return lax.broadcasted_iota(jnp.int32, shape, axis)


def dot(a, b):
    return jnp.dot(a, b, preferred_element_type=jnp.float32)


def as_bf16(mask):
    return mask.astype(jnp.float32).astype(jnp.bfloat16)


def spill_select():
    size = EXPERTS * MAIN
    row, col = iota((size, size), 0), iota((size, size), 1)
    return as_bf16(col == ((row & 63) >> 1) * MAIN + (row >> 6) * SPILL + (row & 1))


def dispatch_kernel(ids_ref, gates_ref, tokens_ref, out_ref, mix_ref, mix_spill_ref, select_ref):
    select_ref[...] = spill_select()
    rows, top = ids_ref.shape
    named = jnp.zeros((rows, EXPERTS), jnp.float32)
    gates = jnp.zeros((rows, EXPERTS), jnp.float32)
    for k in range(top):
        hit = ids_ref[:, k : k + 1] == iota((rows, EXPERTS), 1)
        named = named + hit.astype(jnp.float32)
        gates = gates + jnp.where(hit, gates_ref[:, k : k + 1], 0.0)
    named16 = named.astype(jnp.bfloat16)
    row, col = iota((rows, rows), 0), iota((rows, rows), 1)
    slots = dot(as_bf16(col < row), named16)
    over_tokens = (((0,), (0,)), ((), ()))
    named_t = lax.dot_general(named16, as_bf16(row == col), over_tokens, preferred_element_type=jnp.float32)
    slots_t = lax.dot_general(named16, as_bf16(row < col), over_tokens, preferred_element_type=jnp.float32)
    slots_t = jnp.where(named_t > 0.5, slots_t, -1.0)
    wide = jnp.broadcast_to(slots_t[:, None, :], (EXPERTS, MAIN, rows)).reshape(EXPERTS * MAIN, rows)
    place = iota((EXPERTS * MAIN, rows), 0) % MAIN
    pick = as_bf16(wide == place.astype(jnp.float32))
    width = tokens_ref.shape[1]
    blocks = width // LANES
    for b in range(0, blocks, 2):
        part = dot(pick, tokens_ref[:, b * LANES : (b + 2) * LANES]).astype(jnp.bfloat16)
        for i in range(2):
            out_ref[:, (b + i) * MAIN : (b + i + 1) * MAIN, :] = part[:, i * LANES : (i + 1) * LANES].reshape(
                EXPERTS, MAIN, LANES
            )
    picks = [
        as_bf16((place // SPILL == i) & (wide == (MAIN + place % SPILL).astype(jnp.float32))) for i in range(8)
    ]
    for g in range(blocks // 8):
        part = jnp.zeros((EXPERTS * MAIN, LANES), jnp.float32)
        for i in range(8):
            b = 8 * g + i
            part = part + dot(picks[i], tokens_ref[:, b * LANES : (b + 1) * LANES])
        start = blocks * MAIN + g * MAIN
        out_ref[:, start : start + MAIN, :] = part.astype(jnp.bfloat16).reshape(EXPERTS, MAIN, LANES)
    first = gates.astype(jnp.bfloat16)
    rest = gates - first.astype(jnp.float32)
    second = rest.astype(jnp.bfloat16)
    third = (rest - second.astype(jnp.float32)).astype(jnp.bfloat16)
    slots16 = slots.astype(jnp.bfloat16)
    for ref, per, base in ((mix_ref, MAIN, 0), (mix_spill_ref, SPILL, MAIN)):
        size = EXPERTS * per
        spread = as_bf16(iota((EXPERTS, size), 1) // per == iota((EXPERTS, size), 0))
        fits = dot(slots16, spread) == (base + iota((rows, size), 1) % per).astype(jnp.float32)
        for i, term in enumerate((first, second, third)):
            ref[i * rows : (i + 1) * rows, :] = jnp.where(fits, dot(term, spread), 0.0).astype(jnp.bfloat16)


def dispatch(ids, gates, tokens):
    rows, width = tokens.shape
    return pl.pallas_call(
        dispatch_kernel,
        out_shape=(
            jax.ShapeDtypeStruct((EXPERTS, CAP * width // LANES, LANES), jnp.bfloat16),
            jax.ShapeDtypeStruct((3 * rows, EXPERTS * MAIN), jnp.bfloat16),
            jax.ShapeDtypeStruct((3 * rows, EXPERTS * SPILL), jnp.bfloat16),
            jax.ShapeDtypeStruct((EXPERTS * MAIN, EXPERTS * MAIN), jnp.bfloat16),
        ),
        compiler_params=pltpu.CompilerParams(vmem_limit_bytes=60 * MIB),
    )(ids, gates, tokens)


def unpack_kernel(select_ref, in_ref, out_ref):
    width = out_ref.shape[1]
    blocks = width // LANES
    size = EXPERTS * MAIN
    for b in range(blocks):
        out_ref[:size, b * LANES : (b + 1) * LANES] = in_ref[:, b * MAIN : (b + 1) * MAIN, :].reshape(size, LANES)
    for g in range(blocks // 8):
        start = blocks * MAIN + g * MAIN
        part = dot(select_ref[...], in_ref[:, start : start + MAIN, :].reshape(size, LANES)).astype(jnp.bfloat16)
        for i in range(8):
            b = 8 * g + i
            out_ref[size:, b * LANES : (b + 1) * LANES] = part[i * 64 : (i + 1) * 64]


def unpack(select, incoming):
    width = incoming.shape[1] * LANES // CAP
    return pl.pallas_call(
        unpack_kernel,
        out_shape=jax.ShapeDtypeStruct((EXPERTS * CAP, width), jnp.bfloat16),
        compiler_params=pltpu.CompilerParams(vmem_limit_bytes=60 * MIB),
    )(select, incoming)


def gate_up_kernel(x_ref, gate_ref, up_ref, out_ref):
    gate = dot(x_ref[...], gate_ref[0])
    up = dot(x_ref[...], up_ref[0])
    out_ref[...] = (gate / (1.0 + jnp.exp(-gate)) * up).astype(jnp.bfloat16)


def gate_up_rows(x, weights, step=256):
    rows, width = x.shape
    steps = FF // step
    return pl.pallas_call(
        gate_up_kernel,
        grid=(steps,),
        in_specs=[
            pl.BlockSpec((rows, width), lambda j: (0, 0)),
            pl.BlockSpec((1, width, step), lambda j: (0, 0, j)),
            pl.BlockSpec((1, width, step), lambda j: (0, 0, steps + j)),
        ],
        out_specs=pl.BlockSpec((rows, step), lambda j: (0, j)),
        out_shape=jax.ShapeDtypeStruct((rows, FF), jnp.bfloat16),
        compiler_params=pltpu.CompilerParams(vmem_limit_bytes=60 * MIB),
    )(x, weights, weights)


def down_kernel(places_ref, select_ref, hidden_ref, *refs):
    pieces, (out_ref, held, sems) = refs[:-3], refs[-3:]
    depth = pieces[0].shape[1]
    copies = []
    for i, piece in enumerate(pieces):
        start = pl.multiple_of(places_ref[i] * depth, 32)
        copies.append(pltpu.make_async_copy(piece.at[0], held.at[pl.ds(start, depth), :], sems.at[i]))
        copies[-1].start()
    for copy in copies:
        copy.wait()
    blocks = held.shape[1] // LANES
    size = EXPERTS * MAIN
    for g in range(blocks // 8):
        spill = []
        for p in range(4):
            b = 8 * g + 2 * p
            weights = held[:, b * LANES : (b + 2) * LANES]
            part = dot(hidden_ref[...], weights).astype(jnp.bfloat16)
            for i in range(2):
                out_ref[:, (b + i) * MAIN : (b + i + 1) * MAIN, :] = part[
                    :size, i * LANES : (i + 1) * LANES
                ].reshape(EXPERTS, MAIN, LANES)
                spill.append(part[size:, i * LANES : (i + 1) * LANES])
        start = blocks * MAIN + g * MAIN
        out_ref[:, start : start + MAIN, :] = (
            lax.dot_general(
                select_ref[...],
                jnp.concatenate(spill, axis=0),
                (((0,), (0,)), ((), ())),
                preferred_element_type=jnp.float32,
            )
            .astype(jnp.bfloat16)
            .reshape(EXPERTS, MAIN, LANES)
        )


def down_rows(places, select, hidden, pieces):
    depth, width = pieces[0].shape[1:]
    count = len(pieces)
    return pl.pallas_call(
        down_kernel,
        in_specs=[pl.BlockSpec(memory_space=pltpu.SMEM)]
        + [pl.BlockSpec(memory_space=pltpu.VMEM)] * 2
        + [pl.BlockSpec(memory_space=pl.ANY)] * count,
        out_shape=jax.ShapeDtypeStruct((EXPERTS, CAP * width // LANES, LANES), jnp.bfloat16),
        scratch_shapes=[pltpu.VMEM((count * depth, width), jnp.bfloat16), pltpu.SemaphoreType.DMA((count,))],
        compiler_params=pltpu.CompilerParams(vmem_limit_bytes=60 * MIB),
    )(places, select, hidden, *pieces)


def combine_kernel(mix_ref, mix_spill_ref, select_ref, in_ref, *refs):
    out_ref = refs[-1]
    offset = 0
    if len(refs) == 2:
        offset = refs[0].shape[1]
        out_ref[:, :offset] = refs[0][...]
    blocks = in_ref.shape[1] // CAP
    size = EXPERTS * MAIN
    rows = out_ref.shape[0]
    for g in range(blocks // 8):
        start = blocks * MAIN + g * MAIN
        spill = dot(select_ref[...], in_ref[:, start : start + MAIN, :].reshape(size, LANES)).astype(jnp.bfloat16)
        for p in range(4):
            b = 8 * g + 2 * p
            main = jnp.concatenate(
                [in_ref[:, (b + i) * MAIN : (b + i + 1) * MAIN, :].reshape(size, LANES) for i in range(2)], axis=1
            )
            extra = jnp.concatenate([spill[(2 * p + i) * 64 : (2 * p + i + 1) * 64] for i in range(2)], axis=1)
            total = dot(mix_ref[...], main) + dot(mix_spill_ref[...], extra)
            total = total[2 * rows :] + total[rows : 2 * rows] + total[:rows]
            out_ref[:, offset + b * LANES : offset + (b + 2) * LANES] = total.astype(jnp.bfloat16)


def combine(mix, mix_spill, select, returned, *earlier):
    width = returned.shape[1] * LANES // CAP + sum([e.shape[1] for e in earlier])
    return pl.pallas_call(
        combine_kernel,
        out_shape=jax.ShapeDtypeStruct((mix.shape[0] // 3, width), jnp.bfloat16),
        compiler_params=pltpu.CompilerParams(vmem_limit_bytes=60 * MIB),
    )(mix, mix_spill, select, returned, *earlier)


STEPS = {1: 4, -1: 3}


def tie(value, others):
    return lax.optimization_barrier((value, tuple(others)))[0]


def body(tokens, expert_ids, gate_scale, gate_up, down):
    n, me = lax.axis_size("fsdp"), lax.axis_index("fsdp")
    split = down.shape[2] // 2
    weights = lax.all_gather(gate_up, "fsdp", axis=1, tiled=True)
    gathered = lax.all_gather(down[:, :, split:], "fsdp", axis=1, tiled=True)
    pieces, shards = [down[:, :, :split]], [me]
    latest = {way: pieces[0] for way in STEPS}
    for k in range(1, 5):
        for way, steps in STEPS.items():
            if k <= steps:
                latest[way] = lax.ppermute(latest[way], "fsdp", [(j, (j + way) % n) for j in range(n)])
                pieces.append(latest[way])
                shards.append((me - way * k + n) % n)
    places = jnp.stack(shards).astype(jnp.int32)

    outgoing, mix, mix_spill, select = dispatch(expert_ids, gate_scale, tokens)
    incoming = lax.all_to_all(outgoing, "expert", split_axis=0, concat_axis=0, tiled=True)
    x = unpack(select, incoming)
    hidden = gate_up_rows(tie(x, pieces[1:]), weights)

    result = []
    for places, pieces in ((places, pieces), (jnp.zeros((1,), jnp.int32), [gathered])):
        rows = down_rows(places, select, hidden, pieces)
        returned = lax.all_to_all(rows, "expert", split_axis=0, concat_axis=0, tiled=True)
        result = [combine(mix, mix_spill, select, returned, *result)]
    return result[0]


def solution(mesh):
    return jax.shard_map(
        body,
        mesh=mesh,
        in_specs=(
            P(("fsdp", "expert"), None),
            P(("fsdp", "expert"), None),
            P(("fsdp", "expert"), None),
            P("expert", "fsdp", None),
            P("expert", "fsdp", None),
        ),
        out_specs=P(("fsdp", "expert"), None),
        check_vma=False,
    )
```

```python
import functools

import jax
import jax.numpy as jnp
from jax import lax
from jax.experimental import pallas as pl
from jax.experimental.pallas import tpu as pltpu
from jax.sharding import PartitionSpec as P

FF = 768
EXPERTS = 32
CAP = 18
MAIN = 16
GROUP = 8
SPILL = CAP - MAIN
LANES = 128
MIB = 1024 * 1024


def iota(shape, axis):
    return lax.broadcasted_iota(jnp.int32, shape, axis)


def dot(a, b):
    return jnp.dot(a, b, preferred_element_type=jnp.float32)


def as_bf16(mask):
    return mask.astype(jnp.float32).astype(jnp.bfloat16)


def spill_select(transposed):
    size = EXPERTS * MAIN
    row, col = iota((size, size), 0), iota((size, size), 1)
    if transposed:
        row, col = col, row
    return as_bf16(col == ((row & 63) >> 1) * MAIN + (row >> 6) * SPILL + (row & 1))


def row_of(block):
    return block // GROUP * GROUP * CAP + block % GROUP * MAIN


def spill_row_of(group):
    return group * GROUP * CAP + GROUP * MAIN


def dispatch_kernel(ids_ref, gates_ref, tokens_ref, out_ref, mix_ref, mix_spill_ref, select_ref, pack_ref):
    select_ref[...] = spill_select(False)
    pack_ref[...] = spill_select(True)
    rows, top = ids_ref.shape
    named = jnp.zeros((rows, EXPERTS), jnp.float32)
    gates = jnp.zeros((rows, EXPERTS), jnp.float32)
    for k in range(top):
        hit = ids_ref[:, k : k + 1] == iota((rows, EXPERTS), 1)
        named = named + hit.astype(jnp.float32)
        gates = gates + jnp.where(hit, gates_ref[:, k : k + 1], 0.0)
    named16 = named.astype(jnp.bfloat16)
    row, col = iota((rows, rows), 0), iota((rows, rows), 1)
    slots = dot(as_bf16(col < row), named16)
    over_tokens = (((0,), (0,)), ((), ()))
    named_t = lax.dot_general(named16, as_bf16(row == col), over_tokens, preferred_element_type=jnp.float32)
    slots_t = lax.dot_general(named16, as_bf16(row < col), over_tokens, preferred_element_type=jnp.float32)
    slots_t = jnp.where(named_t > 0.5, slots_t, -1.0)
    wide = jnp.broadcast_to(slots_t[:, None, :], (EXPERTS, MAIN, rows)).reshape(EXPERTS * MAIN, rows)
    place = iota((EXPERTS * MAIN, rows), 0) % MAIN
    pick = as_bf16(wide == place.astype(jnp.float32))
    width = tokens_ref.shape[1]
    blocks = width // LANES
    for b in range(0, blocks, 2):
        part = dot(pick, tokens_ref[:, b * LANES : (b + 2) * LANES]).astype(jnp.bfloat16)
        for i in range(2):
            start = row_of(b + i)
            out_ref[:, start : start + MAIN, :] = part[:, i * LANES : (i + 1) * LANES].reshape(EXPERTS, MAIN, LANES)
    picks = [
        as_bf16((place // SPILL == i) & (wide == (MAIN + place % SPILL).astype(jnp.float32))) for i in range(8)
    ]
    for g in range(blocks // 8):
        part = jnp.zeros((EXPERTS * MAIN, LANES), jnp.float32)
        for i in range(8):
            b = 8 * g + i
            part = part + dot(picks[i], tokens_ref[:, b * LANES : (b + 1) * LANES])
        start = spill_row_of(g)
        out_ref[:, start : start + MAIN, :] = part.astype(jnp.bfloat16).reshape(EXPERTS, MAIN, LANES)
    first = gates.astype(jnp.bfloat16)
    rest = gates - first.astype(jnp.float32)
    second = rest.astype(jnp.bfloat16)
    third = (rest - second.astype(jnp.float32)).astype(jnp.bfloat16)
    slots16 = slots.astype(jnp.bfloat16)
    for ref, per, base in ((mix_ref, MAIN, 0), (mix_spill_ref, SPILL, MAIN)):
        size = EXPERTS * per
        spread = as_bf16(iota((EXPERTS, size), 1) // per == iota((EXPERTS, size), 0))
        fits = dot(slots16, spread) == (base + iota((rows, size), 1) % per).astype(jnp.float32)
        for i, term in enumerate((first, second, third)):
            ref[i * rows : (i + 1) * rows, :] = jnp.where(fits, dot(term, spread), 0.0).astype(jnp.bfloat16)


def dispatch(ids, gates, tokens):
    rows, width = tokens.shape
    return pl.pallas_call(
        dispatch_kernel,
        out_shape=(
            jax.ShapeDtypeStruct((EXPERTS, CAP * width // LANES, LANES), jnp.bfloat16),
            jax.ShapeDtypeStruct((3 * rows, EXPERTS * MAIN), jnp.bfloat16),
            jax.ShapeDtypeStruct((3 * rows, EXPERTS * SPILL), jnp.bfloat16),
        )
        + (jax.ShapeDtypeStruct((EXPERTS * MAIN, EXPERTS * MAIN), jnp.bfloat16),) * 2,
        compiler_params=pltpu.CompilerParams(vmem_limit_bytes=60 * MIB),
    )(ids, gates, tokens)


def unpack_kernel(select_ref, in_ref, out_ref):
    size = EXPERTS * MAIN
    for b in range(GROUP):
        start = row_of(b)
        out_ref[:size, b * LANES : (b + 1) * LANES] = in_ref[:, start : start + MAIN, :].reshape(size, LANES)
    start = spill_row_of(0)
    part = dot(select_ref[...], in_ref[:, start : start + MAIN, :].reshape(size, LANES)).astype(jnp.bfloat16)
    for b in range(GROUP):
        out_ref[size:, b * LANES : (b + 1) * LANES] = part[b * 64 : (b + 1) * 64]


def unpack(select, incoming):
    groups = incoming.shape[1] // (GROUP * CAP)
    rows, step = EXPERTS * CAP, GROUP * LANES
    return pl.pallas_call(
        unpack_kernel,
        grid=(groups,),
        in_specs=[
            pl.BlockSpec(select.shape, lambda g: (0, 0)),
            pl.BlockSpec((EXPERTS, GROUP * CAP, LANES), lambda g: (0, g, 0)),
        ],
        out_specs=pl.BlockSpec((rows, step), lambda g: (0, g)),
        out_shape=jax.ShapeDtypeStruct((rows, groups * step), jnp.bfloat16),
        compiler_params=pltpu.CompilerParams(vmem_limit_bytes=60 * MIB),
    )(select, incoming)


def pack(part, out_ref, select):
    size = EXPERTS * MAIN
    for b in range(GROUP):
        start = row_of(b)
        out_ref[:, start : start + MAIN, :] = part[b // 2][:size, b % 2 * LANES : (b % 2 + 1) * LANES].reshape(
            EXPERTS, MAIN, LANES
        )
    spill = [part[b // 2][size:, b % 2 * LANES : (b % 2 + 1) * LANES] for b in range(GROUP)]
    moved = dot(select, jnp.concatenate(spill, axis=0)).astype(jnp.bfloat16)
    start = spill_row_of(0)
    out_ref[:, start : start + MAIN, :] = moved.reshape(EXPERTS, MAIN, LANES)


def gate_up_kernel(x_ref, weights_ref, hidden_ref, held_x, held, total, sems):
    bounds = [0, 512, 1536, 2560, held.shape[0]]
    chunks = len(bounds) - 1
    copies = []
    for i in range(chunks):
        at = pl.ds(bounds[i], bounds[i + 1] - bounds[i])
        copies.append(pltpu.make_async_copy(x_ref.at[:, at], held_x.at[:, at], sems.at[2 * i]))
        copies.append(pltpu.make_async_copy(weights_ref.at[0, at], held.at[at], sems.at[2 * i + 1]))
    for copy in copies:
        copy.start()
    step = 256
    for i in range(chunks):
        copies[2 * i].wait()
        copies[2 * i + 1].wait()
        at = slice(bounds[i], bounds[i + 1])
        for c in range(0, total.shape[1], step):
            part = dot(held_x[:, at], held[at, c : c + step])
            if i > 0:
                part = part + total[:, c : c + step]
            total[:, c : c + step] = part
    for c in range(0, FF, step):
        gate, up = total[:, c : c + step], total[:, FF + c : FF + c + step]
        hidden_ref[:, c : c + step] = (gate / (1.0 + jnp.exp(-gate)) * up).astype(jnp.bfloat16)


def gate_up_rows(x, weights):
    rows, width = x.shape
    return pl.pallas_call(
        gate_up_kernel,
        in_specs=[pl.BlockSpec(memory_space=pl.ANY)] * 2,
        out_specs=pl.BlockSpec(memory_space=pltpu.VMEM),
        out_shape=jax.ShapeDtypeStruct((rows, FF), jnp.bfloat16),
        scratch_shapes=[
            pltpu.VMEM((rows, width), jnp.bfloat16),
            pltpu.VMEM((width, 2 * FF), jnp.bfloat16),
            pltpu.VMEM((rows, 2 * FF), jnp.float32),
            pltpu.SemaphoreType.DMA((8,)),
        ],
        compiler_params=pltpu.CompilerParams(vmem_limit_bytes=60 * MIB),
    )(x, weights)


def first_kernel(places_ref, select_ref, hidden_ref, *refs):
    pieces, (out_ref, held, made, sems) = refs[:-4], refs[-4:]
    rows = pieces[0].shape[1]
    copies = []
    for i, piece in enumerate(pieces):
        at = pl.ds(pl.multiple_of(places_ref[i] * rows, 32), rows)
        copies.append(pltpu.make_async_copy(piece.at[0], held.at[at], sems.at[i]))
        copies[-1].start()
    for copy in copies:
        copy.wait()
    leaving = []
    for g in range(made.shape[0]):
        part = []
        for p in range(GROUP // 2):
            begin = (g * GROUP + 2 * p) * LANES
            part.append(dot(hidden_ref[...], held[:, begin : begin + 2 * LANES]).astype(jnp.bfloat16))
        pack(part, made.at[g], select_ref[...])
        at = pl.ds(g * GROUP * CAP, GROUP * CAP)
        leaving.append(pltpu.make_async_copy(made.at[g], out_ref.at[:, at], sems.at[len(pieces) + g]))
        leaving[-1].start()
    for copy in leaving:
        copy.wait()


def first_rows(places, select, hidden, pieces):
    depth, columns = pieces[0].shape[1:]
    count, groups = len(pieces), columns // (GROUP * LANES)
    vmem, smem = pl.BlockSpec(memory_space=pltpu.VMEM), pl.BlockSpec(memory_space=pltpu.SMEM)
    return pl.pallas_call(
        first_kernel,
        in_specs=[smem, vmem, vmem] + [pl.BlockSpec(memory_space=pl.ANY)] * count,
        out_specs=pl.BlockSpec(memory_space=pl.ANY),
        out_shape=jax.ShapeDtypeStruct((EXPERTS, groups * GROUP * CAP, LANES), jnp.bfloat16),
        scratch_shapes=[
            pltpu.VMEM((count * depth, columns), jnp.bfloat16),
            pltpu.VMEM((groups, EXPERTS, GROUP * CAP, LANES), jnp.bfloat16),
            pltpu.SemaphoreType.DMA((count + groups,)),
        ],
        compiler_params=pltpu.CompilerParams(vmem_limit_bytes=60 * MIB),
    )(places, select, hidden, *pieces)


def down_kernel(select_ref, hidden_ref, weights_ref, out_ref):
    part = []
    for p in range(GROUP // 2):
        at = slice(2 * p * LANES, (2 * p + 2) * LANES)
        part.append(dot(hidden_ref[...], weights_ref[0, :, at]).astype(jnp.bfloat16))
    pack(part, out_ref, select_ref[...])


def down_rows(select, hidden, weights):
    depth, width = weights.shape[1:]
    step = GROUP * LANES
    return pl.pallas_call(
        down_kernel,
        grid=(width // step,),
        in_specs=[
            pl.BlockSpec(memory_space=pltpu.VMEM),
            pl.BlockSpec(memory_space=pltpu.VMEM),
            pl.BlockSpec((1, depth, step), lambda g: (0, 0, g)),
        ],
        out_specs=pl.BlockSpec((EXPERTS, GROUP * CAP, LANES), lambda g: (0, g, 0)),
        out_shape=jax.ShapeDtypeStruct((EXPERTS, width // LANES * CAP, LANES), jnp.bfloat16),
        compiler_params=pltpu.CompilerParams(vmem_limit_bytes=60 * MIB),
    )(select, hidden, weights)


def combine_kernel(mix_ref, mix_spill_ref, select_ref, in_ref, *refs):
    out_ref = refs[-1]
    size = EXPERTS * MAIN
    rows = out_ref.shape[0]
    start = spill_row_of(0)
    spill = dot(select_ref[...], in_ref[:, start : start + MAIN, :].reshape(size, LANES)).astype(jnp.bfloat16)
    for p in range(GROUP // 2):
        main, extra = [], []
        for b in (2 * p, 2 * p + 1):
            start = row_of(b)
            main.append(in_ref[:, start : start + MAIN, :].reshape(size, LANES))
            extra.append(spill[b * 64 : (b + 1) * 64])
        total = dot(mix_ref[...], jnp.concatenate(main, axis=1))
        total = total + dot(mix_spill_ref[...], jnp.concatenate(extra, axis=1))
        total = total[2 * rows :] + total[rows : 2 * rows] + total[:rows]
        out_ref[:, 2 * p * LANES : (2 * p + 2) * LANES] = total.astype(jnp.bfloat16)


def combine(mix, mix_spill, select, returned, width, first, earlier):
    step = GROUP * LANES
    whole = pl.BlockSpec(memory_space=pltpu.VMEM)
    return pl.pallas_call(
        combine_kernel,
        grid=(returned.shape[1] // (GROUP * CAP),),
        in_specs=[whole] * 3
        + [pl.BlockSpec((EXPERTS, GROUP * CAP, LANES), lambda g: (0, g, 0))]
        + [pl.BlockSpec(memory_space=pl.ANY)] * len(earlier),
        out_specs=pl.BlockSpec((mix.shape[0] // 3, step), lambda g: (0, first + g)),
        out_shape=jax.ShapeDtypeStruct((mix.shape[0] // 3, width), jnp.bfloat16),
        input_output_aliases={4: 0} if earlier else {},
        compiler_params=pltpu.CompilerParams(vmem_limit_bytes=60 * MIB),
    )(mix, mix_spill, select, returned, *earlier)


STEPS = {1: 4, -1: 3}


def tie(value, others):
    return lax.optimization_barrier((value, tuple(others)))[0]


def body(tokens, expert_ids, gate_scale, gate_up, down):
    n, me = lax.axis_size("fsdp"), lax.axis_index("fsdp")
    split = down.shape[2] // 2
    weights = lax.all_gather(gate_up, "fsdp", axis=1, tiled=True)
    gathered = lax.all_gather(down[:, :, split:], "fsdp", axis=1, tiled=True)
    own = down[:, :, :split]
    pieces, shards = [own], [me]
    latest = {way: own for way in STEPS}

    def step(k):
        for way, steps in STEPS.items():
            if k <= steps:
                latest[way] = lax.ppermute(latest[way], "fsdp", [(j, (j + way) % n) for j in range(n)])
                pieces.append(latest[way])
                shards.append((me - way * k + n) % n)

    step(1)
    tokens = tie(tokens, pieces[1:])
    outgoing, mix, mix_spill, select, packing = dispatch(expert_ids, gate_scale, tokens)
    incoming = lax.all_to_all(outgoing, "expert", split_axis=0, concat_axis=0, tiled=True)
    x = unpack(select, incoming)
    step(2)
    step(3)
    weights, x, latest[1] = lax.optimization_barrier((weights, tie(x, pieces[1:]), latest[1]))
    step(4)
    hidden = gate_up_rows(x, weights)

    result = []
    for part in range(2):
        if part == 0:
            rows = first_rows(jnp.stack(shards).astype(jnp.int32), packing, hidden, pieces)
        else:
            rows = down_rows(packing, hidden, gathered)
        returned = lax.all_to_all(rows, "expert", split_axis=0, concat_axis=0, tiled=True)
        first = part * split // (GROUP * LANES)
        result = [combine(mix, mix_spill, select, returned, down.shape[2], first, result)]
    return result[0]


def solution(mesh):
    return jax.shard_map(
        body,
        mesh=mesh,
        in_specs=(
            P(("fsdp", "expert"), None),
            P(("fsdp", "expert"), None),
            P(("fsdp", "expert"), None),
            P("expert", "fsdp", None),
            P("expert", "fsdp", None),
        ),
        out_specs=P(("fsdp", "expert"), None),
        check_vma=False,
    )
```

```python
import functools

import jax
import jax.numpy as jnp
from jax import lax
from jax.experimental import pallas as pl
from jax.experimental.pallas import tpu as pltpu
from jax.sharding import PartitionSpec as P

FF = 768
EXPERTS = 32
CAP = 18
MAIN = 16
GROUP = 8
SPILL = CAP - MAIN
LANES = 128
MIB = 1024 * 1024


def iota(shape, axis):
    return lax.broadcasted_iota(jnp.int32, shape, axis)


def dot(a, b):
    return jnp.dot(a, b, preferred_element_type=jnp.float32)


def as_bf16(mask):
    return mask.astype(jnp.float32).astype(jnp.bfloat16)


def spill_select(transposed):
    size = EXPERTS * MAIN
    row, col = iota((size, size), 0), iota((size, size), 1)
    if transposed:
        row, col = col, row
    return as_bf16(col == ((row & 63) >> 1) * MAIN + (row >> 6) * SPILL + (row & 1))


def row_of(block):
    return block // GROUP * GROUP * CAP + block % GROUP * MAIN


def spill_row_of(group):
    return group * GROUP * CAP + GROUP * MAIN


def dispatch_kernel(ids_ref, gates_ref, tokens_ref, out_ref, mix_ref, mix_spill_ref, select_ref, pack_ref):
    select_ref[...] = spill_select(False)
    pack_ref[...] = spill_select(True)
    rows, top = ids_ref.shape
    named = jnp.zeros((rows, EXPERTS), jnp.float32)
    gates = jnp.zeros((rows, EXPERTS), jnp.float32)
    for k in range(top):
        hit = ids_ref[:, k : k + 1] == iota((rows, EXPERTS), 1)
        named = named + hit.astype(jnp.float32)
        gates = gates + jnp.where(hit, gates_ref[:, k : k + 1], 0.0)
    named16 = named.astype(jnp.bfloat16)
    row, col = iota((rows, rows), 0), iota((rows, rows), 1)
    slots = dot(as_bf16(col < row), named16)
    over_tokens = (((0,), (0,)), ((), ()))
    named_t = lax.dot_general(named16, as_bf16(row == col), over_tokens, preferred_element_type=jnp.float32)
    slots_t = lax.dot_general(named16, as_bf16(row < col), over_tokens, preferred_element_type=jnp.float32)
    slots_t = jnp.where(named_t > 0.5, slots_t, -1.0)
    wide = jnp.broadcast_to(slots_t[:, None, :], (EXPERTS, MAIN, rows)).reshape(EXPERTS * MAIN, rows)
    place = iota((EXPERTS * MAIN, rows), 0) % MAIN
    pick = as_bf16(wide == place.astype(jnp.float32))
    width = tokens_ref.shape[1]
    blocks = width // LANES
    for b in range(0, blocks, 2):
        part = dot(pick, tokens_ref[:, b * LANES : (b + 2) * LANES]).astype(jnp.bfloat16)
        for i in range(2):
            start = row_of(b + i)
            out_ref[:, start : start + MAIN, :] = part[:, i * LANES : (i + 1) * LANES].reshape(EXPERTS, MAIN, LANES)
    picks = [
        as_bf16((place // SPILL == i) & (wide == (MAIN + place % SPILL).astype(jnp.float32))) for i in range(8)
    ]
    for g in range(blocks // 8):
        part = jnp.zeros((EXPERTS * MAIN, LANES), jnp.float32)
        for i in range(8):
            b = 8 * g + i
            part = part + dot(picks[i], tokens_ref[:, b * LANES : (b + 1) * LANES])
        start = spill_row_of(g)
        out_ref[:, start : start + MAIN, :] = part.astype(jnp.bfloat16).reshape(EXPERTS, MAIN, LANES)
    first = gates.astype(jnp.bfloat16)
    rest = gates - first.astype(jnp.float32)
    second = rest.astype(jnp.bfloat16)
    third = (rest - second.astype(jnp.float32)).astype(jnp.bfloat16)
    slots16 = slots.astype(jnp.bfloat16)
    for ref, per, base in ((mix_ref, MAIN, 0), (mix_spill_ref, SPILL, MAIN)):
        size = EXPERTS * per
        spread = as_bf16(iota((EXPERTS, size), 1) // per == iota((EXPERTS, size), 0))
        fits = dot(slots16, spread) == (base + iota((rows, size), 1) % per).astype(jnp.float32)
        for i, term in enumerate((first, second, third)):
            ref[i * rows : (i + 1) * rows, :] = jnp.where(fits, dot(term, spread), 0.0).astype(jnp.bfloat16)


def dispatch(ids, gates, tokens):
    rows, width = tokens.shape
    return pl.pallas_call(
        dispatch_kernel,
        out_shape=(
            jax.ShapeDtypeStruct((EXPERTS, CAP * width // LANES, LANES), jnp.bfloat16),
            jax.ShapeDtypeStruct((3 * rows, EXPERTS * MAIN), jnp.bfloat16),
            jax.ShapeDtypeStruct((3 * rows, EXPERTS * SPILL), jnp.bfloat16),
        )
        + (jax.ShapeDtypeStruct((EXPERTS * MAIN, EXPERTS * MAIN), jnp.bfloat16),) * 2,
        compiler_params=pltpu.CompilerParams(vmem_limit_bytes=60 * MIB),
    )(ids, gates, tokens)


def unpack_kernel(select_ref, in_ref, out_ref):
    size = EXPERTS * MAIN
    for b in range(GROUP):
        start = row_of(b)
        out_ref[:size, b * LANES : (b + 1) * LANES] = in_ref[:, start : start + MAIN, :].reshape(size, LANES)
    start = spill_row_of(0)
    part = dot(select_ref[...], in_ref[:, start : start + MAIN, :].reshape(size, LANES)).astype(jnp.bfloat16)
    for b in range(GROUP):
        out_ref[size:, b * LANES : (b + 1) * LANES] = part[b * 64 : (b + 1) * 64]


def unpack(select, incoming):
    groups = incoming.shape[1] // (GROUP * CAP)
    rows, step = EXPERTS * CAP, GROUP * LANES
    return pl.pallas_call(
        unpack_kernel,
        grid=(groups,),
        in_specs=[
            pl.BlockSpec(select.shape, lambda g: (0, 0)),
            pl.BlockSpec((EXPERTS, GROUP * CAP, LANES), lambda g: (0, g, 0)),
        ],
        out_specs=pl.BlockSpec((rows, step), lambda g: (0, g)),
        out_shape=jax.ShapeDtypeStruct((rows, groups * step), jnp.bfloat16),
        compiler_params=pltpu.CompilerParams(vmem_limit_bytes=60 * MIB),
    )(select, incoming)


def pack(part, out_ref, select):
    size = EXPERTS * MAIN
    for b in range(GROUP):
        start = row_of(b)
        out_ref[:, start : start + MAIN, :] = part[b // 2][:size, b % 2 * LANES : (b % 2 + 1) * LANES].reshape(
            EXPERTS, MAIN, LANES
        )
    spill = [part[b // 2][size:, b % 2 * LANES : (b % 2 + 1) * LANES] for b in range(GROUP)]
    moved = dot(select, jnp.concatenate(spill, axis=0)).astype(jnp.bfloat16)
    start = spill_row_of(0)
    out_ref[:, start : start + MAIN, :] = moved.reshape(EXPERTS, MAIN, LANES)


def gate_up_kernel(x_ref, weights_ref, hidden_ref, held_x, held, total, sems):
    bounds = [0, 256, 1024, 2048, 3072, held.shape[0]]
    chunks = len(bounds) - 1
    copies = []
    for i in range(chunks):
        at = pl.ds(bounds[i], bounds[i + 1] - bounds[i])
        copies.append(pltpu.make_async_copy(x_ref.at[:, at], held_x.at[:, at], sems.at[2 * i]))
        copies.append(pltpu.make_async_copy(weights_ref.at[0, at], held.at[at], sems.at[2 * i + 1]))
    for copy in copies:
        copy.start()
    step = 256
    for i in range(chunks):
        copies[2 * i].wait()
        copies[2 * i + 1].wait()
        at = slice(bounds[i], bounds[i + 1])
        for c in range(0, total.shape[1], step):
            part = dot(held_x[:, at], held[at, c : c + step])
            if i > 0:
                part = part + total[:, c : c + step]
            total[:, c : c + step] = part
    for c in range(0, FF, step):
        gate, up = total[:, c : c + step], total[:, FF + c : FF + c + step]
        hidden_ref[:, c : c + step] = (gate / (1.0 + jnp.exp(-gate)) * up).astype(jnp.bfloat16)


def gate_up_rows(x, weights):
    rows, width = x.shape
    return pl.pallas_call(
        gate_up_kernel,
        in_specs=[pl.BlockSpec(memory_space=pltpu.HBM)] * 2,
        out_specs=pl.BlockSpec(memory_space=pltpu.VMEM),
        out_shape=jax.ShapeDtypeStruct((rows, FF), jnp.bfloat16),
        scratch_shapes=[
            pltpu.VMEM((rows, width), jnp.bfloat16),
            pltpu.VMEM((width, 2 * FF), jnp.bfloat16),
            pltpu.VMEM((rows, 2 * FF), jnp.float32),
            pltpu.SemaphoreType.DMA((10,)),
        ],
        compiler_params=pltpu.CompilerParams(vmem_limit_bytes=60 * MIB),
    )(x, weights)


def first_kernel(places_ref, select_ref, hidden_ref, *refs):
    pieces, (out_ref, held, made, held_hidden, held_select, sems, leave_sems) = refs[:-7], refs[-7:]
    rows, width = pieces[0].shape[1], GROUP * LANES
    groups = made.shape[0]
    hidden_copy = pltpu.make_async_copy(hidden_ref, held_hidden, sems.at[groups, 0])
    select_copy = pltpu.make_async_copy(select_ref, held_select, sems.at[groups, 1])
    hidden_copy.start()
    copies = []
    for g in range(groups):
        cols = pl.ds(g * width, width)
        copies.append([])
        for i, piece in enumerate(pieces):
            at = pl.ds(pl.multiple_of(places_ref[i] * rows, 32), rows)
            copies[g].append(pltpu.make_async_copy(piece.at[0, :, cols], held.at[at, cols], sems.at[g, i]))
            copies[g][-1].start()
        if g == 0:
            select_copy.start()
    leaving = []
    hidden_copy.wait()
    for g in range(groups):
        for copy in copies[g]:
            copy.wait()
        part = []
        for p in range(GROUP // 2):
            begin = (g * GROUP + 2 * p) * LANES
            part.append(dot(held_hidden[...], held[:, begin : begin + 2 * LANES]).astype(jnp.bfloat16))
        if g == 0:
            select_copy.wait()
        pack(part, made.at[g], held_select[...])
        at = pl.ds(g * GROUP * CAP, GROUP * CAP)
        leaving.append(pltpu.make_async_copy(made.at[g], out_ref.at[:, at], leave_sems.at[g]))
        leaving[-1].start()
    for copy in leaving:
        copy.wait()


def first_rows(places, select, hidden, pieces):
    depth, columns = pieces[0].shape[1:]
    count, groups = len(pieces), columns // (GROUP * LANES)
    return pl.pallas_call(
        first_kernel,
        in_specs=[pl.BlockSpec(memory_space=pltpu.SMEM)] + [pl.BlockSpec(memory_space=pl.ANY)] * (2 + count),
        out_specs=pl.BlockSpec(memory_space=pl.ANY),
        out_shape=jax.ShapeDtypeStruct((EXPERTS, groups * GROUP * CAP, LANES), jnp.bfloat16),
        scratch_shapes=[
            pltpu.VMEM((count * depth, columns), jnp.bfloat16),
            pltpu.VMEM((groups, EXPERTS, GROUP * CAP, LANES), jnp.bfloat16),
            pltpu.VMEM(hidden.shape, jnp.bfloat16),
            pltpu.VMEM(select.shape, jnp.bfloat16),
            pltpu.SemaphoreType.DMA((groups + 1, count)),
            pltpu.SemaphoreType.DMA((groups,)),
        ],
        compiler_params=pltpu.CompilerParams(vmem_limit_bytes=60 * MIB),
    )(places, select, hidden, *pieces)


def down_kernel(select_ref, hidden_ref, weights_ref, out_ref):
    part = []
    for p in range(GROUP // 2):
        at = slice(2 * p * LANES, (2 * p + 2) * LANES)
        part.append(dot(hidden_ref[...], weights_ref[0, :, at]).astype(jnp.bfloat16))
    pack(part, out_ref, select_ref[...])


def down_rows(select, hidden, weights):
    depth, width = weights.shape[1:]
    step = GROUP * LANES
    return pl.pallas_call(
        down_kernel,
        grid=(width // step,),
        in_specs=[
            pl.BlockSpec(memory_space=pltpu.VMEM),
            pl.BlockSpec(memory_space=pltpu.VMEM),
            pl.BlockSpec((1, depth, step), lambda g: (0, 0, g)),
        ],
        out_specs=pl.BlockSpec((EXPERTS, GROUP * CAP, LANES), lambda g: (0, g, 0)),
        out_shape=jax.ShapeDtypeStruct((EXPERTS, width // LANES * CAP, LANES), jnp.bfloat16),
        compiler_params=pltpu.CompilerParams(vmem_limit_bytes=60 * MIB),
    )(select, hidden, weights)


def combine_kernel(first, mix_ref, mix_spill_ref, select_ref, in_ref, *refs):
    out_ref, held, made, sems = refs[-4:]
    groups = held.shape[0]
    arriving, leaving = [], []
    for g in range(groups):
        at = pl.ds(g * GROUP * CAP, GROUP * CAP)
        arriving.append(pltpu.make_async_copy(in_ref.at[:, at], held.at[g], sems.at[g]))
        arriving[-1].start()
    size = EXPERTS * MAIN
    rows = made.shape[1]
    for g in range(groups):
        arriving[g].wait()
        start = spill_row_of(0)
        spill = dot(select_ref[...], held[g, :, start : start + MAIN, :].reshape(size, LANES)).astype(jnp.bfloat16)
        for p in range(GROUP // 2):
            main, extra = [], []
            for b in (2 * p, 2 * p + 1):
                start = row_of(b)
                main.append(held[g, :, start : start + MAIN, :].reshape(size, LANES))
                extra.append(spill[b * 64 : (b + 1) * 64])
            total = dot(mix_ref[...], jnp.concatenate(main, axis=1))
            total = total + dot(mix_spill_ref[...], jnp.concatenate(extra, axis=1))
            total = total[2 * rows :] + total[rows : 2 * rows] + total[:rows]
            made[g, :, 2 * p * LANES : (2 * p + 2) * LANES] = total.astype(jnp.bfloat16)
        at = pl.ds((first + g) * GROUP * LANES, GROUP * LANES)
        leaving.append(pltpu.make_async_copy(made.at[g], out_ref.at[:, at], sems.at[groups + g]))
        leaving[-1].start()
    for copy in leaving:
        copy.wait()


def combine(mix, mix_spill, select, returned, width, first, earlier):
    rows, step = mix.shape[0] // 3, GROUP * LANES
    groups = returned.shape[1] // (GROUP * CAP)
    whole, far = pl.BlockSpec(memory_space=pltpu.VMEM), pl.BlockSpec(memory_space=pltpu.HBM)
    return pl.pallas_call(
        functools.partial(combine_kernel, first),
        in_specs=[whole] * 3 + [far] * (1 + len(earlier)),
        out_specs=far,
        out_shape=jax.ShapeDtypeStruct((rows, width), jnp.bfloat16),
        input_output_aliases={4: 0} if earlier else {},
        scratch_shapes=[
            pltpu.VMEM((groups, EXPERTS, GROUP * CAP, LANES), jnp.bfloat16),
            pltpu.VMEM((groups, rows, step), jnp.bfloat16),
            pltpu.SemaphoreType.DMA((2 * groups,)),
        ],
        compiler_params=pltpu.CompilerParams(vmem_limit_bytes=12 * MIB),
    )(mix, mix_spill, select, returned, *earlier)


STEPS = {1: 4, -1: 3}


def tie(value, others):
    return lax.optimization_barrier((value, tuple(others)))[0]


def body(tokens, expert_ids, gate_scale, gate_up, down):
    n, me = lax.axis_size("fsdp"), lax.axis_index("fsdp")
    split = down.shape[2] // 2
    weights = lax.all_gather(gate_up, "fsdp", axis=1, tiled=True)
    gathered = lax.all_gather(down[:, :, split:], "fsdp", axis=1, tiled=True)
    own = down[:, :, :split]
    pieces, latest = [own], {way: own for way in STEPS}
    shards = [me] + [(me - way * k + n) % n for k in range(1, 5) for way in STEPS if k <= STEPS[way]]
    places = jnp.stack(shards).astype(jnp.int32)

    def step(k):
        for way, steps in STEPS.items():
            if k <= steps:
                latest[way] = lax.ppermute(latest[way], "fsdp", [(j, (j + way) % n) for j in range(n)])
                pieces.append(latest[way])

    step(1)
    tokens = tie(tokens, pieces[1:])
    outgoing, mix, mix_spill, select, packing = dispatch(expert_ids, gate_scale, tokens)
    incoming = lax.all_to_all(outgoing, "expert", split_axis=0, concat_axis=0, tiled=True)
    x = unpack(select, incoming)
    step(2)
    step(3)
    x, places = lax.optimization_barrier((tie(x, pieces[1:]), places))
    weights, x, places, latest[1] = lax.optimization_barrier((weights, x, places, latest[1]))
    step(4)
    hidden = gate_up_rows(x, weights)

    result = []
    for part in range(2):
        if part == 0:
            rows = first_rows(places, packing, hidden, pieces)
        else:
            rows = down_rows(packing, hidden, gathered)
        returned = lax.all_to_all(rows, "expert", split_axis=0, concat_axis=0, tiled=True)
        first = part * split // (GROUP * LANES)
        result = [combine(mix, mix_spill, select, returned, down.shape[2], first, result)]
    return result[0]


def solution(mesh):
    return jax.shard_map(
        body,
        mesh=mesh,
        in_specs=(
            P(("fsdp", "expert"), None),
            P(("fsdp", "expert"), None),
            P(("fsdp", "expert"), None),
            P("expert", "fsdp", None),
            P("expert", "fsdp", None),
        ),
        out_specs=P(("fsdp", "expert"), None),
        check_vma=False,
    )
```

```python
import functools

import jax
import jax.numpy as jnp
from jax import lax
from jax.experimental import pallas as pl
from jax.experimental.pallas import tpu as pltpu
from jax.sharding import PartitionSpec as P

FF = 768
EXPERTS = 32
CAP = 18
MAIN = 16
GROUP = 8
SPILL = CAP - MAIN
LANES = 128
MIB = 1024 * 1024


def iota(shape, axis):
    return lax.broadcasted_iota(jnp.int32, shape, axis)


def dot(a, b):
    return jnp.dot(a, b, preferred_element_type=jnp.float32)


def as_bf16(mask):
    return mask.astype(jnp.float32).astype(jnp.bfloat16)


def spill_select(transposed):
    size = EXPERTS * MAIN
    row, col = iota((size, size), 0), iota((size, size), 1)
    if transposed:
        row, col = col, row
    return as_bf16(col == ((row & 63) >> 1) * MAIN + (row >> 6) * SPILL + (row & 1))


def row_of(block):
    return block // GROUP * GROUP * CAP + block % GROUP * MAIN


def spill_row_of(group):
    return group * GROUP * CAP + GROUP * MAIN


def dispatch_kernel(ids_ref, gates_ref, tokens_ref, out_ref, mix_ref, mix_spill_ref, select_ref, pack_ref):
    select_ref[...] = spill_select(False)
    pack_ref[...] = spill_select(True)
    rows, top = ids_ref.shape
    named = jnp.zeros((rows, EXPERTS), jnp.float32)
    gates = jnp.zeros((rows, EXPERTS), jnp.float32)
    for k in range(top):
        hit = ids_ref[:, k : k + 1] == iota((rows, EXPERTS), 1)
        named = named + hit.astype(jnp.float32)
        gates = gates + jnp.where(hit, gates_ref[:, k : k + 1], 0.0)
    named16 = named.astype(jnp.bfloat16)
    row, col = iota((rows, rows), 0), iota((rows, rows), 1)
    slots = dot(as_bf16(col < row), named16)
    over_tokens = (((0,), (0,)), ((), ()))
    named_t = lax.dot_general(named16, as_bf16(row == col), over_tokens, preferred_element_type=jnp.float32)
    slots_t = lax.dot_general(named16, as_bf16(row < col), over_tokens, preferred_element_type=jnp.float32)
    slots_t = jnp.where(named_t > 0.5, slots_t, -1.0)
    wide = jnp.broadcast_to(slots_t[:, None, :], (EXPERTS, MAIN, rows)).reshape(EXPERTS * MAIN, rows)
    place = iota((EXPERTS * MAIN, rows), 0) % MAIN
    pick = as_bf16(wide == place.astype(jnp.float32))
    width = tokens_ref.shape[1]
    blocks = width // LANES
    for b in range(0, blocks, 2):
        part = dot(pick, tokens_ref[:, b * LANES : (b + 2) * LANES]).astype(jnp.bfloat16)
        for i in range(2):
            start = row_of(b + i)
            out_ref[:, start : start + MAIN, :] = part[:, i * LANES : (i + 1) * LANES].reshape(EXPERTS, MAIN, LANES)
    picks = [
        as_bf16((place // SPILL == i) & (wide == (MAIN + place % SPILL).astype(jnp.float32))) for i in range(8)
    ]
    for g in range(blocks // 8):
        part = jnp.zeros((EXPERTS * MAIN, LANES), jnp.float32)
        for i in range(8):
            b = 8 * g + i
            part = part + dot(picks[i], tokens_ref[:, b * LANES : (b + 1) * LANES])
        start = spill_row_of(g)
        out_ref[:, start : start + MAIN, :] = part.astype(jnp.bfloat16).reshape(EXPERTS, MAIN, LANES)
    first = gates.astype(jnp.bfloat16)
    rest = gates - first.astype(jnp.float32)
    second = rest.astype(jnp.bfloat16)
    third = (rest - second.astype(jnp.float32)).astype(jnp.bfloat16)
    slots16 = slots.astype(jnp.bfloat16)
    for ref, per, base in ((mix_ref, MAIN, 0), (mix_spill_ref, SPILL, MAIN)):
        size = EXPERTS * per
        spread = as_bf16(iota((EXPERTS, size), 1) // per == iota((EXPERTS, size), 0))
        fits = dot(slots16, spread) == (base + iota((rows, size), 1) % per).astype(jnp.float32)
        for i, term in enumerate((first, second, third)):
            ref[i * rows : (i + 1) * rows, :] = jnp.where(fits, dot(term, spread), 0.0).astype(jnp.bfloat16)


def dispatch(ids, gates, tokens):
    rows, width = tokens.shape
    return pl.pallas_call(
        dispatch_kernel,
        out_shape=(
            jax.ShapeDtypeStruct((EXPERTS, CAP * width // LANES, LANES), jnp.bfloat16),
            jax.ShapeDtypeStruct((3 * rows, EXPERTS * MAIN), jnp.bfloat16),
            jax.ShapeDtypeStruct((3 * rows, EXPERTS * SPILL), jnp.bfloat16),
        )
        + (jax.ShapeDtypeStruct((EXPERTS * MAIN, EXPERTS * MAIN), jnp.bfloat16),) * 2,
        compiler_params=pltpu.CompilerParams(vmem_limit_bytes=60 * MIB),
    )(ids, gates, tokens)


def unpack_kernel(select_ref, in_ref, out_ref):
    size = EXPERTS * MAIN
    for b in range(GROUP):
        start = row_of(b)
        out_ref[:size, b * LANES : (b + 1) * LANES] = in_ref[:, start : start + MAIN, :].reshape(size, LANES)
    start = spill_row_of(0)
    part = dot(select_ref[...], in_ref[:, start : start + MAIN, :].reshape(size, LANES)).astype(jnp.bfloat16)
    for b in range(GROUP):
        out_ref[size:, b * LANES : (b + 1) * LANES] = part[b * 64 : (b + 1) * 64]


def unpack(select, incoming):
    groups = incoming.shape[1] // (GROUP * CAP)
    rows, step = EXPERTS * CAP, GROUP * LANES
    return pl.pallas_call(
        unpack_kernel,
        grid=(groups,),
        in_specs=[
            pl.BlockSpec(select.shape, lambda g: (0, 0)),
            pl.BlockSpec((EXPERTS, GROUP * CAP, LANES), lambda g: (0, g, 0)),
        ],
        out_specs=pl.BlockSpec((rows, step), lambda g: (0, g)),
        out_shape=jax.ShapeDtypeStruct((rows, groups * step), jnp.bfloat16),
        compiler_params=pltpu.CompilerParams(vmem_limit_bytes=60 * MIB),
    )(select, incoming)


def pack(part, out_ref, select):
    size = EXPERTS * MAIN
    for b in range(GROUP):
        start = row_of(b)
        out_ref[:, start : start + MAIN, :] = part[b // 2][:size, b % 2 * LANES : (b % 2 + 1) * LANES].reshape(
            EXPERTS, MAIN, LANES
        )
    spill = [part[b // 2][size:, b % 2 * LANES : (b % 2 + 1) * LANES] for b in range(GROUP)]
    moved = dot(select, jnp.concatenate(spill, axis=0)).astype(jnp.bfloat16)
    start = spill_row_of(0)
    out_ref[:, start : start + MAIN, :] = moved.reshape(EXPERTS, MAIN, LANES)


def gate_up_kernel(x_ref, weights_ref, hidden_ref, held_x, held, total, sems):
    bounds = [0, 256, 1024, 2048, 3072, held.shape[0]]
    chunks = len(bounds) - 1
    copies = []
    for i in range(chunks):
        at = pl.ds(bounds[i], bounds[i + 1] - bounds[i])
        copies.append(pltpu.make_async_copy(x_ref.at[:, at], held_x.at[:, at], sems.at[2 * i]))
        copies.append(pltpu.make_async_copy(weights_ref.at[0, at], held.at[at], sems.at[2 * i + 1]))
    for copy in copies:
        copy.start()
    step = 256
    for i in range(chunks):
        copies[2 * i].wait()
        copies[2 * i + 1].wait()
        at = slice(bounds[i], bounds[i + 1])
        for c in range(0, total.shape[1], step):
            part = dot(held_x[:, at], held[at, c : c + step])
            if i > 0:
                part = part + total[:, c : c + step]
            total[:, c : c + step] = part
    for c in range(0, FF, step):
        gate, up = total[:, c : c + step], total[:, FF + c : FF + c + step]
        hidden_ref[:, c : c + step] = (gate / (1.0 + jnp.exp(-gate)) * up).astype(jnp.bfloat16)


def gate_up_rows(x, weights):
    rows, width = x.shape
    return pl.pallas_call(
        gate_up_kernel,
        in_specs=[pl.BlockSpec(memory_space=pltpu.HBM)] * 2,
        out_specs=pl.BlockSpec(memory_space=pltpu.VMEM),
        out_shape=jax.ShapeDtypeStruct((rows, FF), jnp.bfloat16),
        scratch_shapes=[
            pltpu.VMEM((rows, width), jnp.bfloat16),
            pltpu.VMEM((width, 2 * FF), jnp.bfloat16),
            pltpu.VMEM((rows, 2 * FF), jnp.float32),
            pltpu.SemaphoreType.DMA((10,)),
        ],
        compiler_params=pltpu.CompilerParams(vmem_limit_bytes=60 * MIB),
    )(x, weights)


def first_kernel(places_ref, select_ref, hidden_ref, *refs):
    pieces, (out_ref, held, made, held_hidden, held_select, sems, leave_sems) = refs[:-7], refs[-7:]
    rows, width = pieces[0].shape[1], GROUP * LANES
    groups = made.shape[0]
    hidden_copy = pltpu.make_async_copy(hidden_ref, held_hidden, sems.at[groups, 0])
    select_copy = pltpu.make_async_copy(select_ref, held_select, sems.at[groups, 1])
    hidden_copy.start()
    copies = []
    for g in range(groups):
        cols = pl.ds(g * width, width)
        copies.append([])
        for i, piece in enumerate(pieces):
            at = pl.ds(pl.multiple_of(places_ref[i] * rows, 32), rows)
            copies[g].append(pltpu.make_async_copy(piece.at[0, :, cols], held.at[at, cols], sems.at[g, i]))
            copies[g][-1].start()
        if g == 0:
            select_copy.start()
    leaving = []
    hidden_copy.wait()
    for g in range(groups):
        for copy in copies[g]:
            copy.wait()
        part = []
        for p in range(GROUP // 2):
            begin = (g * GROUP + 2 * p) * LANES
            part.append(dot(held_hidden[...], held[:, begin : begin + 2 * LANES]).astype(jnp.bfloat16))
        if g == 0:
            select_copy.wait()
        pack(part, made.at[g], held_select[...])
        at = pl.ds(g * GROUP * CAP, GROUP * CAP)
        leaving.append(pltpu.make_async_copy(made.at[g], out_ref.at[:, at], leave_sems.at[g]))
        leaving[-1].start()
    for copy in leaving:
        copy.wait()


def first_rows(places, select, hidden, pieces):
    depth, columns = pieces[0].shape[1:]
    count, groups = len(pieces), columns // (GROUP * LANES)
    return pl.pallas_call(
        first_kernel,
        in_specs=[pl.BlockSpec(memory_space=pltpu.SMEM)] + [pl.BlockSpec(memory_space=pl.ANY)] * (2 + count),
        out_specs=pl.BlockSpec(memory_space=pl.ANY),
        out_shape=jax.ShapeDtypeStruct((EXPERTS, groups * GROUP * CAP, LANES), jnp.bfloat16),
        scratch_shapes=[
            pltpu.VMEM((count * depth, columns), jnp.bfloat16),
            pltpu.VMEM((groups, EXPERTS, GROUP * CAP, LANES), jnp.bfloat16),
            pltpu.VMEM(hidden.shape, jnp.bfloat16),
            pltpu.VMEM(select.shape, jnp.bfloat16),
            pltpu.SemaphoreType.DMA((groups + 1, count)),
            pltpu.SemaphoreType.DMA((groups,)),
        ],
        compiler_params=pltpu.CompilerParams(vmem_limit_bytes=60 * MIB),
    )(places, select, hidden, *pieces)


def down_kernel(select_ref, hidden_ref, weights_ref, out_ref):
    part = []
    for p in range(GROUP // 2):
        at = slice(2 * p * LANES, (2 * p + 2) * LANES)
        part.append(dot(hidden_ref[...], weights_ref[0, :, at]).astype(jnp.bfloat16))
    pack(part, out_ref, select_ref[...])


def down_rows(select, hidden, weights):
    depth, width = weights.shape[1:]
    step = GROUP * LANES
    return pl.pallas_call(
        down_kernel,
        grid=(width // step,),
        in_specs=[
            pl.BlockSpec(memory_space=pltpu.VMEM),
            pl.BlockSpec(memory_space=pltpu.VMEM),
            pl.BlockSpec((1, depth, step), lambda g: (0, 0, g)),
        ],
        out_specs=pl.BlockSpec((EXPERTS, GROUP * CAP, LANES), lambda g: (0, g, 0)),
        out_shape=jax.ShapeDtypeStruct((EXPERTS, width // LANES * CAP, LANES), jnp.bfloat16),
        compiler_params=pltpu.CompilerParams(vmem_limit_bytes=60 * MIB),
    )(select, hidden, weights)


def combine_kernel(first, mix_ref, mix_spill_ref, select_ref, in_ref, *refs):
    out_ref, held, made, sems, leave_sems = refs[-5:]
    groups = held.shape[0]
    parts = [(spill_row_of(0), MAIN)] + [(row_of(b), 2 * MAIN) for b in range(0, GROUP, 2)]
    arriving, leaving = [], []
    for g in range(groups):
        arriving.append([])
        for i, (start, count) in enumerate(parts):
            source = in_ref.at[:, pl.ds(g * GROUP * CAP + start, count)]
            arriving[g].append(pltpu.make_async_copy(source, held.at[g, :, pl.ds(start, count)], sems.at[g, i]))
            arriving[g][-1].start()
    size = EXPERTS * MAIN
    rows = made.shape[1]
    for g in range(groups):
        arriving[g][0].wait()
        start = spill_row_of(0)
        spill = dot(select_ref[...], held[g, :, start : start + MAIN, :].reshape(size, LANES)).astype(jnp.bfloat16)
        for p in range(GROUP // 2):
            arriving[g][1 + p].wait()
            main, extra = [], []
            for b in (2 * p, 2 * p + 1):
                start = row_of(b)
                main.append(held[g, :, start : start + MAIN, :].reshape(size, LANES))
                extra.append(spill[b * 64 : (b + 1) * 64])
            total = dot(mix_ref[...], jnp.concatenate(main, axis=1))
            total = total + dot(mix_spill_ref[...], jnp.concatenate(extra, axis=1))
            total = total[2 * rows :] + total[rows : 2 * rows] + total[:rows]
            made[g, :, 2 * p * LANES : (2 * p + 2) * LANES] = total.astype(jnp.bfloat16)
        at = pl.ds((first + g) * GROUP * LANES, GROUP * LANES)
        leaving.append(pltpu.make_async_copy(made.at[g], out_ref.at[:, at], leave_sems.at[g]))
        leaving[-1].start()
    for copy in leaving:
        copy.wait()


def combine(mix, mix_spill, select, returned, width, first, earlier):
    rows, step = mix.shape[0] // 3, GROUP * LANES
    groups = returned.shape[1] // (GROUP * CAP)
    whole, far = pl.BlockSpec(memory_space=pltpu.VMEM), pl.BlockSpec(memory_space=pltpu.HBM)
    return pl.pallas_call(
        functools.partial(combine_kernel, first),
        in_specs=[whole] * 3 + [far] * (1 + len(earlier)),
        out_specs=far,
        out_shape=jax.ShapeDtypeStruct((rows, width), jnp.bfloat16),
        input_output_aliases={4: 0} if earlier else {},
        scratch_shapes=[
            pltpu.VMEM((groups, EXPERTS, GROUP * CAP, LANES), jnp.bfloat16),
            pltpu.VMEM((groups, rows, step), jnp.bfloat16),
            pltpu.SemaphoreType.DMA((groups, 1 + GROUP // 2)),
            pltpu.SemaphoreType.DMA((groups,)),
        ],
        compiler_params=pltpu.CompilerParams(vmem_limit_bytes=12 * MIB),
    )(mix, mix_spill, select, returned, *earlier)


STEPS = {1: 4, -1: 3}


def tie(value, others):
    return lax.optimization_barrier((value, tuple(others)))[0]


def body(tokens, expert_ids, gate_scale, gate_up, down):
    n, me = lax.axis_size("fsdp"), lax.axis_index("fsdp")
    split = down.shape[2] // 2
    weights = lax.all_gather(gate_up, "fsdp", axis=1, tiled=True)
    gathered = lax.all_gather(down[:, :, split:], "fsdp", axis=1, tiled=True)
    own = down[:, :, :split]
    pieces, latest = [own], {way: own for way in STEPS}
    shards = [me] + [(me - way * k + n) % n for k in range(1, 5) for way in STEPS if k <= STEPS[way]]
    places = jnp.stack(shards).astype(jnp.int32)

    def step(k):
        for way, steps in STEPS.items():
            if k <= steps:
                latest[way] = lax.ppermute(latest[way], "fsdp", [(j, (j + way) % n) for j in range(n)])
                pieces.append(latest[way])

    step(1)
    tokens = tie(tokens, pieces[1:])
    outgoing, mix, mix_spill, select, packing = dispatch(expert_ids, gate_scale, tokens)
    incoming = lax.all_to_all(outgoing, "expert", split_axis=0, concat_axis=0, tiled=True)
    x = unpack(select, incoming)
    step(2)
    step(3)
    x, places = lax.optimization_barrier((tie(x, pieces[1:]), places))
    weights, x, places, latest[1] = lax.optimization_barrier((weights, x, places, latest[1]))
    step(4)
    hidden = gate_up_rows(x, weights)

    result = []
    for part in range(2):
        if part == 0:
            rows = first_rows(places, packing, hidden, pieces)
        else:
            rows = down_rows(packing, hidden, gathered)
        returned = lax.all_to_all(rows, "expert", split_axis=0, concat_axis=0, tiled=True)
        first = part * split // (GROUP * LANES)
        result = [combine(mix, mix_spill, select, returned, down.shape[2], first, result)]
    return result[0]


def solution(mesh):
    return jax.shard_map(
        body,
        mesh=mesh,
        in_specs=(
            P(("fsdp", "expert"), None),
            P(("fsdp", "expert"), None),
            P(("fsdp", "expert"), None),
            P("expert", "fsdp", None),
            P("expert", "fsdp", None),
        ),
        out_specs=P(("fsdp", "expert"), None),
        check_vma=False,
    )
```

```python
import functools

import jax
import jax.numpy as jnp
from jax import lax
from jax.experimental import pallas as pl
from jax.experimental.pallas import tpu as pltpu
from jax.sharding import PartitionSpec as P

FF = 768
EXPERTS = 32
CAP = 18
MAIN = 16
GROUP = 8
SPILL = CAP - MAIN
LANES = 128
MIB = 1024 * 1024


def iota(shape, axis):
    return lax.broadcasted_iota(jnp.int32, shape, axis)


def dot(a, b):
    return jnp.dot(a, b, preferred_element_type=jnp.float32)


def as_bf16(mask):
    return mask.astype(jnp.float32).astype(jnp.bfloat16)


def spill_select(transposed):
    size = EXPERTS * MAIN
    row, col = iota((size, size), 0), iota((size, size), 1)
    if transposed:
        row, col = col, row
    return as_bf16(col == ((row & 63) >> 1) * MAIN + (row >> 6) * SPILL + (row & 1))


def row_of(block):
    return block // GROUP * GROUP * CAP + block % GROUP * MAIN


def spill_row_of(group):
    return group * GROUP * CAP + GROUP * MAIN


def dispatch_kernel(ids_ref, gates_ref, tokens_ref, out_ref, mix_ref, mix_spill_ref, select_ref, pack_ref):
    select_ref[...] = spill_select(False)
    pack_ref[...] = spill_select(True)
    rows, top = ids_ref.shape
    named = jnp.zeros((rows, EXPERTS), jnp.float32)
    gates = jnp.zeros((rows, EXPERTS), jnp.float32)
    for k in range(top):
        hit = ids_ref[:, k : k + 1] == iota((rows, EXPERTS), 1)
        named = named + hit.astype(jnp.float32)
        gates = gates + jnp.where(hit, gates_ref[:, k : k + 1], 0.0)
    named16 = named.astype(jnp.bfloat16)
    row, col = iota((rows, rows), 0), iota((rows, rows), 1)
    slots = dot(as_bf16(col < row), named16)
    over_tokens = (((0,), (0,)), ((), ()))
    named_t = lax.dot_general(named16, as_bf16(row == col), over_tokens, preferred_element_type=jnp.float32)
    slots_t = lax.dot_general(named16, as_bf16(row < col), over_tokens, preferred_element_type=jnp.float32)
    slots_t = jnp.where(named_t > 0.5, slots_t, -1.0)
    wide = jnp.broadcast_to(slots_t[:, None, :], (EXPERTS, MAIN, rows)).reshape(EXPERTS * MAIN, rows)
    place = iota((EXPERTS * MAIN, rows), 0) % MAIN
    pick = as_bf16(wide == place.astype(jnp.float32))
    width = tokens_ref.shape[1]
    blocks = width // LANES
    for b in range(0, blocks, 2):
        part = dot(pick, tokens_ref[:, b * LANES : (b + 2) * LANES]).astype(jnp.bfloat16)
        for i in range(2):
            start = row_of(b + i)
            out_ref[:, start : start + MAIN, :] = part[:, i * LANES : (i + 1) * LANES].reshape(EXPERTS, MAIN, LANES)
    picks = [
        as_bf16((place // SPILL == i) & (wide == (MAIN + place % SPILL).astype(jnp.float32))) for i in range(8)
    ]
    for g in range(blocks // 8):
        part = jnp.zeros((EXPERTS * MAIN, LANES), jnp.float32)
        for i in range(8):
            b = 8 * g + i
            part = part + dot(picks[i], tokens_ref[:, b * LANES : (b + 1) * LANES])
        start = spill_row_of(g)
        out_ref[:, start : start + MAIN, :] = part.astype(jnp.bfloat16).reshape(EXPERTS, MAIN, LANES)
    first = gates.astype(jnp.bfloat16)
    rest = gates - first.astype(jnp.float32)
    second = rest.astype(jnp.bfloat16)
    third = (rest - second.astype(jnp.float32)).astype(jnp.bfloat16)
    slots16 = slots.astype(jnp.bfloat16)
    for ref, per, base in ((mix_ref, MAIN, 0), (mix_spill_ref, SPILL, MAIN)):
        size = EXPERTS * per
        spread = as_bf16(iota((EXPERTS, size), 1) // per == iota((EXPERTS, size), 0))
        fits = dot(slots16, spread) == (base + iota((rows, size), 1) % per).astype(jnp.float32)
        for i, term in enumerate((first, second, third)):
            ref[i * rows : (i + 1) * rows, :] = jnp.where(fits, dot(term, spread), 0.0).astype(jnp.bfloat16)


def dispatch(ids, gates, tokens):
    rows, width = tokens.shape
    return pl.pallas_call(
        dispatch_kernel,
        out_shape=(
            jax.ShapeDtypeStruct((EXPERTS, CAP * width // LANES, LANES), jnp.bfloat16),
            jax.ShapeDtypeStruct((3 * rows, EXPERTS * MAIN), jnp.bfloat16),
            jax.ShapeDtypeStruct((3 * rows, EXPERTS * SPILL), jnp.bfloat16),
        )
        + (jax.ShapeDtypeStruct((EXPERTS * MAIN, EXPERTS * MAIN), jnp.bfloat16),) * 2,
        compiler_params=pltpu.CompilerParams(vmem_limit_bytes=60 * MIB),
    )(ids, gates, tokens)


def unpack_kernel(select_ref, in_ref, out_ref):
    size = EXPERTS * MAIN
    for b in range(GROUP):
        start = row_of(b)
        out_ref[:size, b * LANES : (b + 1) * LANES] = in_ref[:, start : start + MAIN, :].reshape(size, LANES)
    start = spill_row_of(0)
    part = dot(select_ref[...], in_ref[:, start : start + MAIN, :].reshape(size, LANES)).astype(jnp.bfloat16)
    for b in range(GROUP):
        out_ref[size:, b * LANES : (b + 1) * LANES] = part[b * 64 : (b + 1) * 64]


def unpack(select, incoming):
    groups = incoming.shape[1] // (GROUP * CAP)
    rows, step = EXPERTS * CAP, GROUP * LANES
    return pl.pallas_call(
        unpack_kernel,
        grid=(groups,),
        in_specs=[
            pl.BlockSpec(select.shape, lambda g: (0, 0)),
            pl.BlockSpec((EXPERTS, GROUP * CAP, LANES), lambda g: (0, g, 0)),
        ],
        out_specs=pl.BlockSpec((rows, step), lambda g: (0, g)),
        out_shape=jax.ShapeDtypeStruct((rows, groups * step), jnp.bfloat16),
        compiler_params=pltpu.CompilerParams(vmem_limit_bytes=60 * MIB),
    )(select, incoming)


def pack(part, out_ref, select):
    size = EXPERTS * MAIN
    for b in range(GROUP):
        start = row_of(b)
        out_ref[:, start : start + MAIN, :] = part[b // 2][:size, b % 2 * LANES : (b % 2 + 1) * LANES].reshape(
            EXPERTS, MAIN, LANES
        )
    spill = [part[b // 2][size:, b % 2 * LANES : (b % 2 + 1) * LANES] for b in range(GROUP)]
    moved = dot(select, jnp.concatenate(spill, axis=0)).astype(jnp.bfloat16)
    start = spill_row_of(0)
    out_ref[:, start : start + MAIN, :] = moved.reshape(EXPERTS, MAIN, LANES)


def gate_up_kernel(x_ref, weights_ref, hidden_ref, held_x, held, total, sems):
    bounds = [0, 256, 1024, 2048, 3072, held.shape[0]]
    chunks = len(bounds) - 1
    copies = []
    for i in range(chunks):
        at = pl.ds(bounds[i], bounds[i + 1] - bounds[i])
        copies.append(pltpu.make_async_copy(x_ref.at[:, at], held_x.at[:, at], sems.at[2 * i]))
        copies.append(pltpu.make_async_copy(weights_ref.at[0, at], held.at[at], sems.at[2 * i + 1]))
    for copy in copies:
        copy.start()
    step = 256
    for i in range(chunks):
        copies[2 * i].wait()
        copies[2 * i + 1].wait()
        at = slice(bounds[i], bounds[i + 1])
        for c in range(0, total.shape[1], step):
            part = dot(held_x[:, at], held[at, c : c + step])
            if i > 0:
                part = part + total[:, c : c + step]
            total[:, c : c + step] = part
    for c in range(0, FF, step):
        gate, up = total[:, c : c + step], total[:, FF + c : FF + c + step]
        hidden_ref[:, c : c + step] = (gate / (1.0 + jnp.exp(-gate)) * up).astype(jnp.bfloat16)


def gate_up_rows(x, weights):
    rows, width = x.shape
    return pl.pallas_call(
        gate_up_kernel,
        in_specs=[pl.BlockSpec(memory_space=pltpu.HBM)] * 2,
        out_specs=pl.BlockSpec(memory_space=pltpu.VMEM),
        out_shape=jax.ShapeDtypeStruct((rows, FF), jnp.bfloat16),
        scratch_shapes=[
            pltpu.VMEM((rows, width), jnp.bfloat16),
            pltpu.VMEM((width, 2 * FF), jnp.bfloat16),
            pltpu.VMEM((rows, 2 * FF), jnp.float32),
            pltpu.SemaphoreType.DMA((10,)),
        ],
        compiler_params=pltpu.CompilerParams(vmem_limit_bytes=60 * MIB),
    )(x, weights)


def first_kernel(places_ref, select_ref, hidden_ref, *refs):
    pieces, (out_ref, held, made, held_hidden, held_select, sems, leave_sems) = refs[:-7], refs[-7:]
    rows, width = pieces[0].shape[1], GROUP * LANES
    groups = made.shape[0]
    hidden_copy = pltpu.make_async_copy(hidden_ref, held_hidden, sems.at[groups, 0])
    select_copy = pltpu.make_async_copy(select_ref, held_select, sems.at[groups, 1])
    hidden_copy.start()
    copies = []
    for g in range(groups):
        cols = pl.ds(g * width, width)
        copies.append([])
        for i, piece in enumerate(pieces):
            at = pl.ds(pl.multiple_of(places_ref[i] * rows, 32), rows)
            copies[g].append(pltpu.make_async_copy(piece.at[0, :, cols], held.at[at, cols], sems.at[g, i]))
            copies[g][-1].start()
        if g == 0:
            select_copy.start()
    leaving = []
    hidden_copy.wait()
    for g in range(groups):
        for copy in copies[g]:
            copy.wait()
        part = []
        for p in range(GROUP // 2):
            begin = (g * GROUP + 2 * p) * LANES
            part.append(dot(held_hidden[...], held[:, begin : begin + 2 * LANES]).astype(jnp.bfloat16))
        if g == 0:
            select_copy.wait()
        pack(part, made.at[g], held_select[...])
        at = pl.ds(g * GROUP * CAP, GROUP * CAP)
        leaving.append(pltpu.make_async_copy(made.at[g], out_ref.at[:, at], leave_sems.at[g]))
        leaving[-1].start()
    for copy in leaving:
        copy.wait()


def first_rows(places, select, hidden, pieces):
    depth, columns = pieces[0].shape[1:]
    count, groups = len(pieces), columns // (GROUP * LANES)
    return pl.pallas_call(
        first_kernel,
        in_specs=[pl.BlockSpec(memory_space=pltpu.SMEM)] + [pl.BlockSpec(memory_space=pl.ANY)] * (2 + count),
        out_specs=pl.BlockSpec(memory_space=pl.ANY),
        out_shape=jax.ShapeDtypeStruct((EXPERTS, groups * GROUP * CAP, LANES), jnp.bfloat16),
        scratch_shapes=[
            pltpu.VMEM((count * depth, columns), jnp.bfloat16),
            pltpu.VMEM((groups, EXPERTS, GROUP * CAP, LANES), jnp.bfloat16),
            pltpu.VMEM(hidden.shape, jnp.bfloat16),
            pltpu.VMEM(select.shape, jnp.bfloat16),
            pltpu.SemaphoreType.DMA((groups + 1, count)),
            pltpu.SemaphoreType.DMA((groups,)),
        ],
        compiler_params=pltpu.CompilerParams(vmem_limit_bytes=60 * MIB),
    )(places, select, hidden, *pieces)


def down_kernel(select_ref, hidden_ref, weights_ref, out_ref):
    part = []
    for p in range(GROUP // 2):
        at = slice(2 * p * LANES, (2 * p + 2) * LANES)
        part.append(dot(hidden_ref[...], weights_ref[0, :, at]).astype(jnp.bfloat16))
    pack(part, out_ref, select_ref[...])


def down_rows(select, hidden, weights):
    depth, width = weights.shape[1:]
    step = GROUP * LANES
    return pl.pallas_call(
        down_kernel,
        grid=(width // step,),
        in_specs=[
            pl.BlockSpec(memory_space=pltpu.VMEM),
            pl.BlockSpec(memory_space=pltpu.VMEM),
            pl.BlockSpec((1, depth, step), lambda g: (0, 0, g)),
        ],
        out_specs=pl.BlockSpec((EXPERTS, GROUP * CAP, LANES), lambda g: (0, g, 0)),
        out_shape=jax.ShapeDtypeStruct((EXPERTS, width // LANES * CAP, LANES), jnp.bfloat16),
        compiler_params=pltpu.CompilerParams(vmem_limit_bytes=60 * MIB),
    )(select, hidden, weights)


def combine_kernel(first, mix_ref, mix_spill_ref, select_ref, in_ref, *refs):
    out_ref, held, made, sems = refs[-4:]
    groups = made.shape[0]
    leaving = []
    arriving = pltpu.make_async_copy(in_ref, held, sems.at[groups])
    arriving.start()
    arriving.wait()
    size = EXPERTS * MAIN
    rows = made.shape[1]
    for g in range(groups):
        start = spill_row_of(g)
        spill = dot(select_ref[...], held[:, start : start + MAIN, :].reshape(size, LANES)).astype(jnp.bfloat16)
        for p in range(GROUP // 2):
            main, extra = [], []
            for b in (2 * p, 2 * p + 1):
                start = row_of(g * GROUP + b)
                main.append(held[:, start : start + MAIN, :].reshape(size, LANES))
                extra.append(spill[b * 64 : (b + 1) * 64])
            total = dot(mix_ref[...], jnp.concatenate(main, axis=1))
            total = total + dot(mix_spill_ref[...], jnp.concatenate(extra, axis=1))
            total = total[2 * rows :] + total[rows : 2 * rows] + total[:rows]
            made[g, :, 2 * p * LANES : (2 * p + 2) * LANES] = total.astype(jnp.bfloat16)
        at = pl.ds((first + g) * GROUP * LANES, GROUP * LANES)
        leaving.append(pltpu.make_async_copy(made.at[g], out_ref.at[:, at], sems.at[g]))
        leaving[-1].start()
    for copy in leaving:
        copy.wait()


def combine(mix, mix_spill, select, returned, width, first, earlier):
    rows, step = mix.shape[0] // 3, GROUP * LANES
    groups = returned.shape[1] // (GROUP * CAP)
    whole, far = pl.BlockSpec(memory_space=pltpu.VMEM), pl.BlockSpec(memory_space=pltpu.HBM)
    return pl.pallas_call(
        functools.partial(combine_kernel, first),
        in_specs=[whole] * 3 + [far] * (1 + len(earlier)),
        out_specs=far,
        out_shape=jax.ShapeDtypeStruct((rows, width), jnp.bfloat16),
        input_output_aliases={4: 0} if earlier else {},
        scratch_shapes=[
            pltpu.VMEM(returned.shape, jnp.bfloat16),
            pltpu.VMEM((groups, rows, step), jnp.bfloat16),
            pltpu.SemaphoreType.DMA((groups + 1,)),
        ],
        compiler_params=pltpu.CompilerParams(vmem_limit_bytes=12 * MIB),
    )(mix, mix_spill, select, returned, *earlier)


STEPS = {1: 4, -1: 3}


def tie(value, others):
    return lax.optimization_barrier((value, tuple(others)))[0]


def body(tokens, expert_ids, gate_scale, gate_up, down):
    n, me = lax.axis_size("fsdp"), lax.axis_index("fsdp")
    split = down.shape[2] // 2
    weights = lax.all_gather(gate_up, "fsdp", axis=1, tiled=True)
    gathered = lax.all_gather(down[:, :, split:], "fsdp", axis=1, tiled=True)
    own = down[:, :, :split]
    pieces, latest = [own], {way: own for way in STEPS}
    shards = [me] + [(me - way * k + n) % n for k in range(1, 5) for way in STEPS if k <= STEPS[way]]
    places = jnp.stack(shards).astype(jnp.int32)

    def step(k):
        for way, steps in STEPS.items():
            if k <= steps:
                latest[way] = lax.ppermute(latest[way], "fsdp", [(j, (j + way) % n) for j in range(n)])
                pieces.append(latest[way])

    step(1)
    tokens = tie(tokens, pieces[1:])
    outgoing, mix, mix_spill, select, packing = dispatch(expert_ids, gate_scale, tokens)
    incoming = lax.all_to_all(outgoing, "expert", split_axis=0, concat_axis=0, tiled=True)
    x = unpack(select, incoming)
    step(2)
    step(3)
    x, places = lax.optimization_barrier((tie(x, pieces[1:]), places))
    weights, x, places, latest[1] = lax.optimization_barrier((weights, x, places, latest[1]))
    step(4)
    hidden = gate_up_rows(x, weights)

    result = []
    for part in range(2):
        if part == 0:
            rows = first_rows(places, packing, hidden, pieces)
        else:
            rows = down_rows(packing, hidden, gathered)
        returned = lax.all_to_all(rows, "expert", split_axis=0, concat_axis=0, tiled=True)
        first = part * split // (GROUP * LANES)
        result = [combine(mix, mix_spill, select, returned, down.shape[2], first, result)]
    return result[0]


def solution(mesh):
    return jax.shard_map(
        body,
        mesh=mesh,
        in_specs=(
            P(("fsdp", "expert"), None),
            P(("fsdp", "expert"), None),
            P(("fsdp", "expert"), None),
            P("expert", "fsdp", None),
            P("expert", "fsdp", None),
        ),
        out_specs=P(("fsdp", "expert"), None),
        check_vma=False,
    )
```
